512 devices in a mesh: outer: 32 (over x, z_lo, core), inner: 16 (over z_hi, y).
Axes of the slice: x: 4, y: 4, z: 16 (z_hi: 4, z_lo: 4; z = z_hi * 4 + z_lo), core: 2. Of those that a mesh axis runs over, the one named last changes fastest.
Arguments:
- hidden: bfloat16 [4096, 8192], P('inner', 'outer'), may hold values from -0.5 to 0.5
- grad_out: bfloat16 [4096, 12288], P('inner', 'outer'), may hold values from -6 to 6
- weight_codes: bfloat16 [8192, 12288], P('outer', 'inner'), may hold values from -1 to 1
- weight_scales: bfloat16 [8192, 48], P('outer', 'inner'), may hold values from 0.0039978027 to 0.029907227
Outputs:
- grad_hidden: bfloat16 [4096, 8192], P('inner', 'outer')
- weight_grad: float32 [8192, 12288], P('outer', 'inner')
The draws below stay inside these ranges and needn't reach their ends.
All inputs are finite; a program needn't handle non-finite values. Where the reference program divides by a largest or mean magnitude, that divisor is 1e-20 or more.
Results may differ from the reference program's by a relative error of at most 0.007.
Values may be sent and summed in bfloat16 or wider, within the bound.
No kernel may reach another device: no remote copies, remote signals or barrier semaphores. Data moves between devices by JAX's collectives and lax.ppermute only.
A program may use at most 128 MiB of HBM per device.

```python
import math
import jax
import jax.numpy as jnp
from jax import lax

D = 12288
TOK_DEV = 256
QBLOCK = 256
HEADW = 8192
TOKENS = 4096
N_INNER = 16


def raised(drawn, stream_key, source, target, blocks, factor):
    owner, partner = [(jnp.arange(drawn.shape[dim]) // (drawn.shape[dim] // blocks)).reshape([-1 if axis == dim else 1 for axis in range(drawn.ndim)]) for dim in (source, target)]
    chosen = jax.random.permutation(stream_key, blocks)[partner]
    strong = (owner == chosen) | (owner == (partner + blocks // 2) % blocks)
    return jnp.where(strong, factor * drawn, drawn)


def block_levels(key, shape, split, least, largest):
    def one(axis_at, blocks):
        draws = jax.random.uniform(jax.random.fold_in(jax.random.fold_in(key, 6), axis_at), (blocks,), jnp.float32, least / len(split), largest / len(split))
        return jnp.repeat(jnp.exp(draws), shape[axis_at] // blocks).reshape((-1,) + (1,) * (len(shape) - axis_at - 1))

    level = one(*split[0])
    for cut in split[1:]:
        level = level * one(*cut)
    return level


def gaussian_with(rng, extent, scale, most, pieces, heavy, held_as=jnp.bfloat16):
    values = scale * jax.random.normal(rng, extent, jnp.float32)
    if pieces:
        values = values * block_levels(rng, extent, pieces, -0.22, 0.18)
    return jnp.clip(raised(values, jax.random.fold_in(rng, 3), *heavy), -most, most).astype(held_as)


def setup_inputs(seed: int = 0) -> dict:
    arg_keys = jax.random.split(jax.random.key(seed), 5)
    return {
        "hidden": gaussian_with(arg_keys[0], (TOKENS, HEADW), 0.02, 0.5, ((0, 16), (1, 32)), (0, 1, 32, 2.75)),
        "grad_out": gaussian_with(arg_keys[1], (TOKENS, D), 1.0, 6.0, ((0, 16), (1, 32)), (0, 1, 32, 2.75)),
        "weight_codes": jnp.clip(jax.random.uniform(arg_keys[2], (HEADW, D), jnp.float32, -1.0, 1.0) * block_levels(arg_keys[2], (HEADW, D), ((0, 32), (1, 16)), -0.4, 0.0), -1.0, 1.0).astype(jnp.bfloat16),
        "weight_scales": jnp.clip(jnp.exp(math.log(0.029907227) - 2.01235525 * jax.random.uniform(arg_keys[3], (HEADW, D // QBLOCK), jnp.float32) ** block_levels(arg_keys[3], (HEADW, D // QBLOCK), ((0, 32), (1, 16)), -0.2, 0.2)), 0.0039978027, 0.029907227).astype(jnp.bfloat16),
    }


def quantize(gradient):
    block_scale = (jnp.max(jnp.abs(gradient), axis=-1) + 1e-6).astype(jnp.bfloat16)
    code_vals = (gradient / block_scale.astype(jnp.float32)[..., None]).astype(jnp.bfloat16)
    return code_vals, block_scale


def expand(code_vals, block_scale):
    return code_vals.astype(jnp.float32) * block_scale.astype(jnp.float32)[..., None]


def reference(hidden, grad_out, weight_codes, weight_scales):
    block_count = D // QBLOCK
    weight = expand(weight_codes.reshape(HEADW, block_count, QBLOCK), weight_scales)
    weight = weight.reshape(HEADW, D).astype(jnp.bfloat16)
    grad_hidden = jnp.dot(grad_out, weight.T, preferred_element_type=jnp.float32).astype(jnp.bfloat16)
    hidden_parts = hidden.reshape(N_INNER, TOK_DEV, HEADW)
    grad_parts = grad_out.reshape(N_INNER, TOK_DEV, D)
    zero_block = jnp.zeros((HEADW, block_count, QBLOCK), jnp.float32)

    def add_member(running, member):
        member_hidden, member_grad = member
        partial_value = jnp.dot(member_hidden.T, member_grad, preferred_element_type=jnp.float32)
        code_vals, block_scale = quantize(partial_value.reshape(HEADW, block_count, QBLOCK))
        return running + expand(code_vals, block_scale), None

    weight_grad, _ = lax.scan(add_member, zero_block, (hidden_parts, grad_parts))
    return grad_hidden, weight_grad.reshape(HEADW, D)
```

```python
import jax
import jax.numpy as jnp
from jax import lax
from jax.experimental import pallas as pl
from jax.experimental.pallas import tpu as pltpu
from jax.sharding import PartitionSpec as P

QBLOCK = 256
NX, NZL, NC, NZH, NY = 4, 4, 2, 4, 4


def transposed_pairs():
    pairs = []
    for a in range(NX):
        for b in range(NZL):
            for c in range(NC):
                for p in range(NZH):
                    for q in range(NY):
                        dz, dy = (p - a) % NZH, (q - b) % NY
                        x, zl = (dz + dy) % NX, dy
                        src = ((a * NZL + b) * NC + c) * (NZH * NY) + p * NY + q
                        dst = ((x * NZL + zl) * NC + c) * (NZH * NY) + a * NY + b
                        pairs.append((src, dst))
    return pairs


def token_blocks():
    j = lax.axis_index("inner")
    zh, y = j // NY, j % NY
    k = jnp.arange(NX * NZL, dtype=jnp.int32)
    x, zl = k // NZL, k % NZL
    return (((zh + x - zl + NZH) % NZH) * NY + (y + zl) % NY).astype(jnp.int32)


def hidden_grad_kernel(idx_ref, grad_ref, weight_ref, out_ref):
    half = grad_ref.shape[-1]
    total = lax.dot_general(grad_ref[0], weight_ref[:, :half], (((1,), (1,)), ((), ())), preferred_element_type=jnp.float32)
    total += lax.dot_general(grad_ref[1], weight_ref[:, half:], (((1,), (1,)), ((), ())), preferred_element_type=jnp.float32)
    out_ref[0] = total.astype(out_ref.dtype)


def hidden_grad_parts(idx, grads, weight):
    n, _, t, half = grads.shape
    f = weight.shape[0]
    return pl.pallas_call(
        hidden_grad_kernel,
        out_shape=jax.ShapeDtypeStruct((n, t, f), jnp.bfloat16),
        grid_spec=pltpu.PrefetchScalarGridSpec(
            num_scalar_prefetch=1,
            grid=(n,),
            in_specs=[
                pl.BlockSpec((None, 2, t, half), lambda i, idx: (i, 0, 0, 0)),
                pl.BlockSpec((f, 2 * half), lambda i, idx: (0, 0)),
            ],
            out_specs=pl.BlockSpec((1, t, f), lambda i, idx: (idx[i], 0, 0)),
        ),
        compiler_params=pltpu.CompilerParams(vmem_limit_bytes=32 * 1024 * 1024),
        cost_estimate=pl.CostEstimate(flops=4 * n * t * f * half, bytes_accessed=4 * n * t * half + 2 * n * t * f, transcendentals=0),
    )(idx, grads, weight)


def weight_grad_kernel(idx_ref, hidden_ref, grad_ref, out_ref):
    @pl.when(pl.program_id(0) == 0)
    def _():
        out_ref[...] = jnp.zeros_like(out_ref)

    grad = jnp.concatenate([grad_ref[0], grad_ref[1]], axis=1)
    part = lax.dot_general(hidden_ref[...], grad, (((0,), (0,)), ((), ())), preferred_element_type=jnp.float32)
    for k in range(part.shape[1] // QBLOCK):
        cols = slice(k * QBLOCK, (k + 1) * QBLOCK)
        g = part[:, cols]
        s = (jnp.max(jnp.abs(g), axis=1, keepdims=True) + 1e-6).astype(jnp.bfloat16).astype(jnp.float32)
        codes = (g * (1.0 / s)).astype(jnp.bfloat16)
        out_ref[:, cols] += codes.astype(jnp.float32) * s


def weight_grad_sum(idx, hidden, grads):
    n, _, t, half = grads.shape
    f = hidden.shape[-1]
    return pl.pallas_call(
        weight_grad_kernel,
        out_shape=jax.ShapeDtypeStruct((f, 2 * half), jnp.float32),
        grid_spec=pltpu.PrefetchScalarGridSpec(
            num_scalar_prefetch=1,
            grid=(n,),
            in_specs=[
                pl.BlockSpec((None, t, f), lambda i, idx: (idx[i], 0, 0)),
                pl.BlockSpec((None, 2, t, half), lambda i, idx: (i, 0, 0, 0)),
            ],
            out_specs=pl.BlockSpec((f, 2 * half), lambda i, idx: (0, 0)),
        ),
        compiler_params=pltpu.CompilerParams(vmem_limit_bytes=32 * 1024 * 1024),
        cost_estimate=pl.CostEstimate(flops=4 * n * t * f * half, bytes_accessed=4 * n * t * half + 2 * n * t * f, transcendentals=0),
    )(idx, hidden, grads)


def local(hidden, grad_out, weight_codes, weight_scales):
    f, width = weight_codes.shape
    idx = token_blocks()
    moved = lax.ppermute(grad_out, ("outer", "inner"), transposed_pairs())
    grads = lax.all_gather(moved, "outer", axis=0)
    grads = grads.reshape(NX * NZL, NC, *moved.shape)
    all_hidden = lax.all_gather(hidden, "inner", axis=0)
    codes = weight_codes.reshape(f, width // QBLOCK, QBLOCK).astype(jnp.float32)
    weight = (codes * weight_scales.astype(jnp.float32)[..., None]).astype(jnp.bfloat16).reshape(f, width)
    parts = hidden_grad_parts(idx, grads, weight)
    got = lax.all_to_all(parts, "inner", split_axis=0, concat_axis=0, tiled=True)
    grad_hidden = jnp.sum(got.astype(jnp.float32), axis=0).astype(jnp.bfloat16)
    weight_grad = weight_grad_sum(idx, all_hidden, grads)
    return grad_hidden, weight_grad


def solution(mesh):
    placed = (P("inner", "outer"), P("inner", "outer"), P("outer", "inner"), P("outer", "inner"))
    return jax.shard_map(
        local,
        mesh=mesh,
        in_specs=placed,
        out_specs=(P("inner", "outer"), P("outer", "inner")),
        check_vma=False,
    )
```

```python
import itertools

import jax
import jax.numpy as jnp
from jax import lax
from jax.experimental import pallas as pl
from jax.experimental.pallas import tpu as pltpu
from jax.sharding import Mesh, PartitionSpec as P

QBLOCK = 256
SIZES = {"x": 4, "zl": 4, "c": 2, "zh": 4, "y": 4}
OUTER, INNER = ("x", "zl", "c"), ("zh", "y")
MiB = 1024 * 1024


def move(value, axes, where):
    def flat(at):
        index = 0
        for a in axes:
            index = index * SIZES[a] + at[a] % SIZES[a]
        return index

    pairs = []
    for spot in itertools.product(*[range(SIZES[a]) for a in axes]):
        at = dict(zip(axes, spot))
        pairs.append((flat(at), flat({**at, **where(at)})))
    return lax.ppermute(value, axes, pairs)


def forward(at):
    return 1 if at["c"] == 0 else -1


def transpose_owner(grad):
    grad = move(grad, ("x", "zl", "zh", "y"), lambda at: {"x": at["x"] - at["zh"] - at["y"] + at["zl"]})
    return move(
        grad,
        ("x", "zl", "zh", "y"),
        lambda at: {"zl": at["y"] - at["zl"], "zh": at["x"] + at["zh"] + at["y"] - at["zl"], "y": at["zl"]},
    )


def gather_tokens(grad):
    spread = jnp.broadcast_to(grad[None], (SIZES["zl"],) + grad.shape)
    mine = lax.all_to_all(spread, "zl", split_axis=0, concat_axis=0, tiled=True)
    back = move(mine, ("x", "c"), lambda at: {"x": at["x"] + forward(at)})
    ahead = move(mine, ("x", "c"), lambda at: {"x": at["x"] - forward(at)})
    far = move(back, ("x", "c"), lambda at: {"x": at["x"] + forward(at)})
    own = [mine, back, ahead, far]
    other = [move(v, ("c",), lambda at: {"c": 1 - at["c"]}) for v in own]
    other = [other[0], other[2], other[1], other[3]]
    return own, other


def positions():
    x, c = lax.axis_index("x"), lax.axis_index("c")
    fwd = 1 - 2 * c
    x_of = [x, x - fwd, x + fwd, x + 2]
    return jnp.stack([v % 4 for v in x_of] + [c, lax.axis_index("zh"), lax.axis_index("y")]).astype(jnp.int32)


def dot(a, b, dims):
    return lax.dot_general(a, b, (dims, ((), ())), preferred_element_type=jnp.float32)


def hidden_grad_kernel(at_ref, *refs):
    pieces, weight_ref, out_ref = refs[:8], refs[8], refs[9]
    g, c = pl.program_id(0), at_ref[4]
    for k in range(4):
        dz = (8 - at_ref[k] - g) % 4
        total = dot(pieces[k][...], weight_ref[0], ((1,), (1,)))
        total += dot(pieces[4 + k][...], weight_ref[1], ((1,), (1,)))
        out_ref[dz] = total.astype(out_ref.dtype)


def piece_spec(t, half):
    return pl.BlockSpec((None, t, half), lambda g, at: (g, 0, 0))


def hidden_grad_parts(at, own, other, weight):
    n, t, half = own[0].shape
    f = weight.shape[1]
    return pl.pallas_call(
        hidden_grad_kernel,
        out_shape=jax.ShapeDtypeStruct((n, 4, t, f), jnp.bfloat16),
        grid_spec=pltpu.PrefetchScalarGridSpec(
            num_scalar_prefetch=1,
            grid=(n,),
            in_specs=[piece_spec(t, half)] * 8 + [pl.BlockSpec((2, f, half), lambda g, at: (0, 0, 0))],
            out_specs=pl.BlockSpec((None, 4, t, f), lambda g, at: ((at[6] + g) % 4, 0, 0, 0)),
        ),
        compiler_params=pltpu.CompilerParams(vmem_limit_bytes=32 * MiB),
        cost_estimate=pl.CostEstimate(flops=64 * t * f * half, bytes_accessed=64 * t * half + 32 * t * f, transcendentals=0),
    )(at, *own, *other, weight)


def weight_grad_kernel(at_ref, hidden_ref, *refs):
    pieces, out_ref = refs[:8], refs[8]
    g, c = pl.program_id(0), at_ref[4]

    @pl.when(g == 0)
    def _():
        out_ref[...] = jnp.zeros_like(out_ref)

    for k in range(4):
        zh = (at_ref[5] + 8 - at_ref[k] - g) % 4
        own, other = pieces[k][...], pieces[4 + k][...]
        low = jnp.where(c == 0, own, other)
        high = jnp.where(c == 0, other, own)
        grad = jnp.concatenate([low, high], axis=1)
        part = dot(hidden_ref[zh], grad, ((0,), (0,)))
        for b in range(part.shape[1] // QBLOCK):
            cols = slice(b * QBLOCK, (b + 1) * QBLOCK)
            value = part[:, cols]
            s = (jnp.max(jnp.abs(value), axis=1, keepdims=True) + 1e-6).astype(jnp.bfloat16).astype(jnp.float32)
            codes = (value * (1.0 / s)).astype(jnp.bfloat16)
            out_ref[:, cols] += codes.astype(jnp.float32) * s


def weight_grad_sum(at, hidden, own, other):
    n, t, half = own[0].shape
    f = hidden.shape[-1]
    return pl.pallas_call(
        weight_grad_kernel,
        out_shape=jax.ShapeDtypeStruct((f, 2 * half), jnp.float32),
        grid_spec=pltpu.PrefetchScalarGridSpec(
            num_scalar_prefetch=1,
            grid=(n,),
            in_specs=[pl.BlockSpec((None, 4, t, f), lambda g, at: ((at[6] + g) % 4, 0, 0, 0))] + [piece_spec(t, half)] * 8,
            out_specs=pl.BlockSpec((f, 2 * half), lambda g, at: (0, 0)),
        ),
        compiler_params=pltpu.CompilerParams(vmem_limit_bytes=32 * MiB),
        cost_estimate=pl.CostEstimate(flops=64 * t * f * half, bytes_accessed=64 * t * half + 32 * t * f, transcendentals=0),
    )(at, hidden, *own, *other)


def sum_over_inner(parts):
    got = lax.all_to_all(parts, "y", split_axis=0, concat_axis=0, tiled=True)
    total = jnp.sum(got.astype(jnp.float32), axis=0)
    first = lax.axis_index("c") == 0
    axes = ("c", "zh")
    ahead = jnp.where(first, total[1], total[3])
    back = jnp.where(first, total[3], total[1])
    from_ahead = move(back.astype(jnp.bfloat16), axes, lambda at: {"zh": at["zh"] - forward(at)})
    passing = move(total[2].astype(jnp.bfloat16), axes, lambda at: {"zh": at["zh"] + forward(at)})
    ahead = (ahead + passing.astype(jnp.float32)).astype(jnp.bfloat16)
    from_back = move(ahead, axes, lambda at: {"zh": at["zh"] + forward(at)})
    return (total[0] + from_back.astype(jnp.float32) + from_ahead.astype(jnp.float32)).astype(jnp.bfloat16)


def local(hidden, grad_out, weight_codes, weight_scales):
    f, width = weight_codes.shape
    at = positions()
    all_hidden = lax.all_gather(lax.all_gather(hidden, "zh", axis=0), "y", axis=0)
    own, other = gather_tokens(transpose_owner(grad_out))
    codes = weight_codes.reshape(f, width // QBLOCK, QBLOCK).astype(jnp.float32)
    weight = (codes * weight_scales.astype(jnp.float32)[..., None]).astype(jnp.bfloat16).reshape(f, width)
    halves = weight.reshape(f, 2, width // 2).swapaxes(0, 1)
    halves = jnp.where(lax.axis_index("c") == 0, halves, halves[::-1])
    grad_hidden = sum_over_inner(hidden_grad_parts(at, own, other, halves))
    weight_grad = weight_grad_sum(at, all_hidden, own, other)
    return grad_hidden, weight_grad


def solution(mesh):
    parts = Mesh(mesh.devices.reshape(tuple(SIZES.values())), tuple(SIZES))
    return jax.shard_map(
        local,
        mesh=parts,
        in_specs=(P(INNER, OUTER), P(INNER, OUTER), P(OUTER, INNER), P(OUTER, INNER)),
        out_specs=(P(INNER, OUTER), P(OUTER, INNER)),
        check_vma=False,
    )
```

```python
import functools
import itertools

import jax
import jax.numpy as jnp
from jax import lax
from jax.experimental import pallas as pl
from jax.experimental.pallas import tpu as pltpu
from jax.sharding import Mesh, PartitionSpec as P

QBLOCK = 256
SIZES = {"x": 4, "zl": 4, "c": 2, "zh": 4, "y": 4}
OUTER, INNER = ("x", "zl", "c"), ("zh", "y")
MiB = 1024 * 1024


def move(value, axes, where):
    def flat(at):
        index = 0
        for a in axes:
            index = index * SIZES[a] + at[a] % SIZES[a]
        return index

    pairs = []
    for spot in itertools.product(*[range(SIZES[a]) for a in axes]):
        at = dict(zip(axes, spot))
        pairs.append((flat(at), flat({**at, **where(at)})))
    return lax.ppermute(value, axes, pairs)


def forward(at):
    return 1 if at["c"] == 0 else -1


def transpose_owner(grad):
    grad = move(grad, ("x", "zl", "zh", "y"), lambda at: {"x": at["x"] - at["zh"] - at["y"] + at["zl"]})
    return move(
        grad,
        ("x", "zl", "zh", "y"),
        lambda at: {"zl": at["y"] - at["zl"], "zh": at["x"] + at["zh"] + at["y"] - at["zl"], "y": at["zl"]},
    )


def gather_hidden(hidden):
    axes = ("c", "zh")
    back = move(hidden, axes, lambda at: {"zh": at["zh"] + forward(at)})
    ahead = move(hidden, axes, lambda at: {"zh": at["zh"] - forward(at)})
    far = move(back, axes, lambda at: {"zh": at["zh"] + forward(at)})
    return back, ahead, far


def positions():
    x, c = lax.axis_index("x"), lax.axis_index("c")
    fwd = 1 - 2 * c
    x_of = [x, x - fwd, x + fwd, x + 2]
    return jnp.stack([v % 4 for v in x_of] + [c, lax.axis_index("zh"), lax.axis_index("y")]).astype(jnp.int32)


def dot(a, b, dims):
    return lax.dot_general(a, b, (dims, ((), ())), preferred_element_type=jnp.float32)


def weight_kernel(at_ref, codes_ref, scales_ref, out_ref):
    half, c = out_ref.shape[-1], at_ref[4]
    cols = []
    for b in range(codes_ref.shape[1] // QBLOCK):
        scale = scales_ref[:, b : b + 1].astype(jnp.float32)
        cols.append((codes_ref[:, b * QBLOCK : (b + 1) * QBLOCK].astype(jnp.float32) * scale).astype(out_ref.dtype))
    weight = jnp.concatenate(cols, axis=1)
    out_ref[c] = weight[:, :half]
    out_ref[1 - c] = weight[:, half:]


SMEM = pl.BlockSpec(memory_space=pltpu.SMEM)
VMEM = pl.BlockSpec(memory_space=pltpu.VMEM)
LIMIT = pltpu.CompilerParams(vmem_limit_bytes=32 * MiB)


def weight_halves(at, codes, scales):
    f, width = codes.shape
    return pl.pallas_call(
        weight_kernel,
        out_shape=jax.ShapeDtypeStruct((2, f, width // 2), jnp.bfloat16),
        in_specs=[SMEM, VMEM, VMEM],
        out_specs=VMEM,
        compiler_params=LIMIT,
    )(at, codes, scales)


def hidden_grad_kernel(count, at_ref, *refs):
    own, other, weight_ref, out_ref = refs[:count], refs[count : 2 * count], refs[2 * count], refs[2 * count + 1]
    for i in range(count):
        for g in range(own[i].shape[0]):
            total = dot(own[i][g], weight_ref[0], ((1,), (1,)))
            total += dot(other[i][g], weight_ref[1], ((1,), (1,)))
            out_ref[(at_ref[6] + g) % 4, i] = total.astype(out_ref.dtype)


def hidden_grad_parts(at, own, other, weight):
    n, t, half = own[0].shape
    f, count = weight.shape[1], len(own)
    return pl.pallas_call(
        functools.partial(hidden_grad_kernel, count),
        out_shape=jax.ShapeDtypeStruct((n, count, t, f), jnp.bfloat16),
        in_specs=[SMEM] + [VMEM] * (2 * count + 1),
        out_specs=VMEM,
        compiler_params=LIMIT,
        cost_estimate=pl.CostEstimate(
            flops=4 * count * n * t * f * half, bytes_accessed=4 * count * n * t * half, transcendentals=0
        ),
    )(at, *own, *other, weight)


def sum_kernel(at_ref, first_ref, middle_ref, last_ref, keep_ref, ahead_ref, back_ref, pass_ref):
    c, y = at_ref[4], at_ref[6]

    def total(dz):
        source = [(y + dz + at_ref[k]) % 4 for k in range(4)]
        parts = [first_ref[source[0], 0], middle_ref[source[1], 0], middle_ref[source[2], 1], last_ref[source[3], 0]]
        low, high = [parts[k].astype(jnp.float32) + parts[k + 1].astype(jnp.float32) for k in (0, 2)]
        return low + high

    pass_ref[...] = total(2).astype(pass_ref.dtype)
    back_ref[...] = total(3 - 2 * c).astype(back_ref.dtype)
    ahead_ref[...] = total(1 + 2 * c)
    keep_ref[...] = total(0)


def sum_parts(at, first, middle, last):
    shape = first.shape[2:]
    wide, narrow = jax.ShapeDtypeStruct(shape, jnp.float32), jax.ShapeDtypeStruct(shape, jnp.bfloat16)
    return pl.pallas_call(
        sum_kernel,
        out_shape=(wide, wide, narrow, narrow),
        in_specs=[SMEM] + [VMEM] * 3,
        out_specs=(VMEM,) * 4,
        compiler_params=LIMIT,
    )(at, first, middle, last)


def piece_spec(t, half):
    return pl.BlockSpec((None, t, half), lambda g, at: (g, 0, 0))


def weight_grad_kernel(at_ref, hidden_ref, *refs):
    pieces, out_ref = refs[:8], refs[8]
    g, c = pl.program_id(0), at_ref[4]

    @pl.when(g == 0)
    def _():
        out_ref[...] = jnp.zeros_like(out_ref)

    for k in range(4):
        dz = (8 - at_ref[k] - g) % 4
        place = jnp.where(dz == 0, 0, jnp.where(dz == 2, 3, jnp.where(dz == 1, 2 - c, 1 + c)))
        own, other = pieces[k][...], pieces[4 + k][...]
        low = jnp.where(c == 0, own, other)
        high = jnp.where(c == 0, other, own)
        grad = jnp.concatenate([low, high], axis=1)
        part = dot(hidden_ref[place], grad, ((0,), (0,)))
        for b in range(part.shape[1] // QBLOCK):
            cols = slice(b * QBLOCK, (b + 1) * QBLOCK)
            value = part[:, cols]
            s = (jnp.max(jnp.abs(value), axis=1, keepdims=True) + 1e-6).astype(jnp.bfloat16).astype(jnp.float32)
            codes = (value * (1.0 / s)).astype(jnp.bfloat16)
            out_ref[:, cols] += codes.astype(jnp.float32) * s


def weight_grad_sum(at, hidden, own, other):
    n, t, half = own[0].shape
    f = hidden.shape[-1]
    return pl.pallas_call(
        weight_grad_kernel,
        out_shape=jax.ShapeDtypeStruct((f, 2 * half), jnp.float32),
        grid_spec=pltpu.PrefetchScalarGridSpec(
            num_scalar_prefetch=1,
            grid=(n,),
            in_specs=[pl.BlockSpec((None, 4, t, f), lambda g, at: ((at[6] + g) % 4, 0, 0, 0))] + [piece_spec(t, half)] * 8,
            out_specs=pl.BlockSpec((f, 2 * half), lambda g, at: (0, 0)),
        ),
        compiler_params=pltpu.CompilerParams(vmem_limit_bytes=32 * MiB),
        cost_estimate=pl.CostEstimate(flops=64 * t * f * half, bytes_accessed=64 * t * half + 32 * t * f, transcendentals=0),
    )(at, hidden, *own, *other)


def over_y(parts):
    return lax.all_to_all(parts, "y", split_axis=0, concat_axis=0, tiled=True)


def sum_over_zh(keep, ahead, back, passing):
    axes = ("c", "zh")
    passing = move(passing, axes, lambda at: {"zh": at["zh"] + forward(at)})
    from_ahead = move(back, axes, lambda at: {"zh": at["zh"] - forward(at)})
    ahead = (ahead + passing.astype(jnp.float32)).astype(jnp.bfloat16)
    from_back = move(ahead, axes, lambda at: {"zh": at["zh"] + forward(at)})
    return (keep + from_back.astype(jnp.float32) + from_ahead.astype(jnp.float32)).astype(jnp.bfloat16)


def local(hidden, grad_out, weight_codes, weight_scales):
    at = positions()
    weight = weight_halves(at, weight_codes, weight_scales)

    hidden_back, hidden_ahead, hidden_far = gather_hidden(hidden)
    grad = transpose_owner(grad_out)
    grad, hidden_back, hidden_ahead = lax.optimization_barrier((grad, hidden_back, hidden_ahead))
    spread = jnp.broadcast_to(grad[None], (SIZES["zl"],) + grad.shape)
    mine = lax.all_to_all(spread, "zl", split_axis=0, concat_axis=0, tiled=True)
    mine, hidden_far = lax.optimization_barrier((mine, hidden_far))
    all_hidden = lax.all_gather(jnp.stack([hidden, hidden_back, hidden_ahead, hidden_far]), "y", axis=0)

    axes = ("x", "c")
    swap = lambda v: move(v, ("c",), lambda at: {"c": 1 - at["c"]})
    back = move(mine, axes, lambda at: {"x": at["x"] + forward(at)})
    ahead = move(mine, axes, lambda at: {"x": at["x"] - forward(at)})
    mine_other = swap(mine)
    first = over_y(hidden_grad_parts(at, [mine], [mine_other], weight))
    far = move(back, axes, lambda at: {"x": at["x"] + forward(at)})
    ahead_other, back_other = swap(back), swap(ahead)
    middle = over_y(hidden_grad_parts(at, [back, ahead], [back_other, ahead_other], weight))
    far_other = swap(far)
    last = over_y(hidden_grad_parts(at, [far], [far_other], weight))

    grad_hidden = sum_over_zh(*sum_parts(at, first, middle, last))
    own, other = [mine, back, ahead, far], [mine_other, back_other, ahead_other, far_other]
    weight_grad = weight_grad_sum(at, all_hidden, own, other)
    return grad_hidden, weight_grad


def solution(mesh):
    parts = Mesh(mesh.devices.reshape(tuple(SIZES.values())), tuple(SIZES))
    return jax.shard_map(
        local,
        mesh=parts,
        in_specs=(P(INNER, OUTER), P(INNER, OUTER), P(OUTER, INNER), P(OUTER, INNER)),
        out_specs=(P(INNER, OUTER), P(OUTER, INNER)),
        check_vma=False,
    )
```

```python
import functools
import itertools

import jax
import jax.numpy as jnp
from jax import lax
from jax.experimental import pallas as pl
from jax.experimental.pallas import tpu as pltpu
from jax.sharding import Mesh, PartitionSpec as P

QBLOCK = 256
SIZES = {"x": 4, "zl": 4, "c": 2, "zh": 4, "y": 4}
OUTER, INNER = ("x", "zl", "c"), ("zh", "y")
MiB = 1024 * 1024


def move(value, axes, where):
    def flat(at):
        index = 0
        for a in axes:
            index = index * SIZES[a] + at[a] % SIZES[a]
        return index

    pairs = []
    for spot in itertools.product(*[range(SIZES[a]) for a in axes]):
        at = dict(zip(axes, spot))
        pairs.append((flat(at), flat({**at, **where(at)})))
    return lax.ppermute(value, axes, pairs)


def forward(at):
    return 1 if at["c"] == 0 else -1


TOKENS = ("x", "zl", "zh", "y")


def spread_over_x(grad):
    return move(grad, TOKENS, lambda at: {"x": at["x"] + at["zh"] + at["y"]})


def transpose_owner(grad):
    return move(
        grad,
        TOKENS,
        lambda at: {"zl": at["zl"] + at["y"], "zh": at["x"] - at["zh"] - at["y"], "y": at["zl"]},
    )


def positions():
    x, c = lax.axis_index("x"), lax.axis_index("c")
    fwd = 1 - 2 * c
    x_of = [x, x - fwd, x + fwd, x + 2]
    return jnp.stack(
        [(v + 4) % 4 for v in x_of] + [c, lax.axis_index("zh"), lax.axis_index("y")]
    ).astype(jnp.int32)


def dot(a, b, dims):
    return lax.dot_general(a, b, (dims, ((), ())), preferred_element_type=jnp.float32)


def weight_kernel(at_ref, codes_ref, scales_ref, out_ref):
    half, c = out_ref.shape[-1], at_ref[4]
    cols = []
    for b in range(codes_ref.shape[1] // QBLOCK):
        scale = scales_ref[:, b : b + 1].astype(jnp.float32)
        cols.append((codes_ref[:, b * QBLOCK : (b + 1) * QBLOCK].astype(jnp.float32) * scale).astype(out_ref.dtype))
    weight = jnp.concatenate(cols, axis=1)
    out_ref[c] = weight[:, :half]
    out_ref[1 - c] = weight[:, half:]


SMEM = pl.BlockSpec(memory_space=pltpu.SMEM)
VMEM = pl.BlockSpec(memory_space=pltpu.VMEM)
LIMIT = pltpu.CompilerParams(vmem_limit_bytes=16 * MiB)


def weight_halves(at, codes, scales):
    f, width = codes.shape
    return pl.pallas_call(
        weight_kernel,
        out_shape=jax.ShapeDtypeStruct((2, f, width // 2), jnp.bfloat16),
        in_specs=[SMEM, VMEM, VMEM],
        out_specs=VMEM,
        compiler_params=LIMIT,
    )(at, codes, scales)


def hidden_grad_kernel(at_ref, own_ref, other_ref, weight_ref, out_ref):
    for g in range(own_ref.shape[0]):
        q = (g + 4 - at_ref[6]) % 4
        for x in range(weight_ref.shape[0]):
            total = dot(own_ref[g], weight_ref[x, 0], ((1,), (1,)))
            total += dot(other_ref[g], weight_ref[x, 1], ((1,), (1,)))
            out_ref[q, x] = total.astype(out_ref.dtype)


def hidden_grad_parts(at, own, other, weight):
    n, t, half = own.shape
    nx, _, f, _ = weight.shape
    return pl.pallas_call(
        hidden_grad_kernel,
        out_shape=jax.ShapeDtypeStruct((n, nx, t, f), jnp.bfloat16),
        in_specs=[SMEM] + [VMEM] * 3,
        out_specs=VMEM,
        compiler_params=LIMIT,
        cost_estimate=pl.CostEstimate(
            flops=4 * nx * n * t * f * half, bytes_accessed=4 * n * t * half, transcendentals=0
        ),
    )(at, own, other, weight)


def sum_y_kernel(got_ref, out_ref):
    for x in range(got_ref.shape[1]):
        parts = [got_ref[k, x].astype(jnp.float32) for k in range(4)]
        out_ref[x] = ((parts[0] + parts[1]) + (parts[2] + parts[3])).astype(out_ref.dtype)


def sum_y(got):
    return pl.pallas_call(
        sum_y_kernel,
        out_shape=jax.ShapeDtypeStruct(got.shape[1:], got.dtype),
        in_specs=[VMEM],
        out_specs=VMEM,
        compiler_params=LIMIT,
    )(got)


def by_distance_kernel(at_ref, got_ref, keep_ref, ahead_ref, back_ref, pass_ref):
    c, zh, y = at_ref[4], at_ref[5], at_ref[6]
    for dz, ref in ((0, keep_ref), (1 + 2 * c, ahead_ref), (3 - 2 * c, back_ref), (2, pass_ref)):
        ref[...] = got_ref[(2 * zh + dz + y) % 4]


def by_distance(at, got):
    block = jax.ShapeDtypeStruct(got.shape[1:], got.dtype)
    return pl.pallas_call(
        by_distance_kernel,
        out_shape=(block,) * 4,
        in_specs=[SMEM, VMEM],
        out_specs=(VMEM,) * 4,
        compiler_params=LIMIT,
    )(at, got)


def add_kernel(*refs):
    total = refs[0][...].astype(jnp.float32)
    for ref in refs[1:-1]:
        total += ref[...].astype(jnp.float32)
    refs[-1][...] = total.astype(refs[-1].dtype)


def add(*terms):
    return pl.pallas_call(
        add_kernel,
        out_shape=jax.ShapeDtypeStruct(terms[0].shape, terms[0].dtype),
        in_specs=[VMEM] * len(terms),
        out_specs=VMEM,
        compiler_params=LIMIT,
    )(*terms)


def piece_spec(t, half):
    return pl.BlockSpec((None, t, half), lambda g, at: (g, 0, 0))


def weight_grad_kernel(count, at_ref, near_ref, far_ref, *refs):
    pieces, out_ref = refs[:-1], refs[-1]
    g, c, zh, y = pl.program_id(0), at_ref[4], at_ref[5], at_ref[6]
    q = (g + 4 - y) % 4

    @pl.when(g == 0)
    def _():
        out_ref[...] = jnp.zeros_like(out_ref)

    for k in range(count):
        dz = (at_ref[k] + 12 - 2 * zh - q) % 4
        place = jnp.where(dz == 0, 0, jnp.where(dz == 2, 3, jnp.where(dz == 1, 2 - c, 1 + c)))
        hidden = jnp.where(place < 2, near_ref[place % 2], far_ref[place % 2])
        own, other = pieces[k][...], pieces[count + k][...]
        low = jnp.where(c == 0, own, other)
        high = jnp.where(c == 0, other, own)
        grad = jnp.concatenate([low, high], axis=1)
        part = dot(hidden, grad, ((0,), (0,)))
        for b in range(part.shape[1] // QBLOCK):
            cols = slice(b * QBLOCK, (b + 1) * QBLOCK)
            value = part[:, cols]
            s = (jnp.max(jnp.abs(value), axis=1, keepdims=True) + 1e-6).astype(jnp.bfloat16).astype(jnp.float32)
            codes = (value * (1.0 / s)).astype(jnp.bfloat16)
            out_ref[:, cols] += codes.astype(jnp.float32) * s


def weight_grad_sum(at, near, far, own, other):
    n, t, half = own[0].shape
    f, count = far.shape[-1], len(own)
    whole = pl.BlockSpec((f, 2 * half), lambda g, at: (0, 0))
    return pl.pallas_call(
        functools.partial(weight_grad_kernel, count),
        out_shape=jax.ShapeDtypeStruct((f, 2 * half), jnp.float32),
        grid_spec=pltpu.PrefetchScalarGridSpec(
            num_scalar_prefetch=1,
            grid=(n,),
            in_specs=[
                pl.BlockSpec((None, 2, t, f), lambda g, at: ((g + 4 - at[6]) % 4, 0, 0, 0)),
                pl.BlockSpec((None, 2, t, f), lambda g, at: ((g + 4 - at[6]) % 4, 0, 0, 0)),
            ]
            + [piece_spec(t, half)] * (2 * count),
            out_specs=whole,
        ),
        compiler_params=LIMIT,
        cost_estimate=pl.CostEstimate(
            flops=4 * count * n * t * f * half, bytes_accessed=4 * count * n * t * half, transcendentals=0
        ),
    )(at, near, far, *own, *other)


def after(value, *others):
    return lax.optimization_barrier((value, *others))[0]


def local(hidden, grad_out, weight_codes, weight_scales):
    at = positions()
    swap = lambda v: move(v, ("c",), lambda at: {"c": 1 - at["c"]})
    along = lambda v, axis, sign: move(
        v, ("c", axis) if axis != "x" else ("x", "c"), lambda at: {axis: at[axis] + sign * forward(at)}
    )
    exchange = lambda v, axis: lax.all_to_all(v, axis, split_axis=0, concat_axis=0, tiled=True)

    halves = weight_halves(at, weight_codes, weight_scales)
    weight = lax.all_gather(halves, "x", axis=0)
    hidden_back = along(hidden, "zh", 1)
    near = lax.all_gather(jnp.stack([hidden, hidden_back]), "y", axis=0)
    grad = transpose_owner(after(spread_over_x(grad_out), halves))
    grad = after(grad, hidden_back)
    mine = exchange(jnp.broadcast_to(grad[None], (SIZES["zl"],) + grad.shape), "zl")
    mine, weight = lax.optimization_barrier((mine, weight))
    mine_other = swap(mine)

    parts = hidden_grad_parts(at, mine, mine_other, weight)
    hidden_ahead = along(after(hidden, parts), "zh", -1)
    hidden_far = along(after(hidden_back, parts), "zh", 1)
    far = lax.all_gather(jnp.stack([hidden_ahead, hidden_far]), "y", axis=0)
    got, near = lax.optimization_barrier((exchange(parts, "y"), near))
    sums = sum_y(got)
    keep, ahead, back, passing = by_distance(at, exchange(sums, "x"))
    passing = along(passing, "zh", 1)
    from_ahead = along(back, "zh", -1)

    piece = after(mine, parts)
    x_back, x_ahead = along(piece, "x", 1), along(piece, "x", -1)
    x_far = along(x_back, "x", 1)
    ahead_other, back_other, far_other = swap(after(x_back, sums)), swap(after(x_ahead, sums)), swap(after(x_far, sums))
    own, other = [mine, x_back, x_ahead, x_far], [mine_other, back_other, ahead_other, far_other]
    weight_grad = weight_grad_sum(at, near, far, own, other)

    from_back = along(add(ahead, passing), "zh", 1)
    from_ahead, weight_grad = lax.optimization_barrier((from_ahead, weight_grad))
    return add(keep, from_back, from_ahead), weight_grad


def solution(mesh):
    parts = Mesh(mesh.devices.reshape(tuple(SIZES.values())), tuple(SIZES))
    return jax.shard_map(
        local,
        mesh=parts,
        in_specs=(P(INNER, OUTER), P(INNER, OUTER), P(OUTER, INNER), P(OUTER, INNER)),
        out_specs=(P(INNER, OUTER), P(OUTER, INNER)),
        check_vma=False,
    )
```

```python
import itertools

import jax
import jax.numpy as jnp
from jax import lax
from jax.experimental import pallas as pl
from jax.experimental.pallas import tpu as pltpu
from jax.sharding import Mesh, PartitionSpec as P

QBLOCK = 256
SIZES = {"x": 4, "zl": 4, "c": 2, "zh": 4, "y": 4}
OUTER, INNER = ("x", "zl", "c"), ("zh", "y")
MiB = 1024 * 1024


def move(value, axes, where):
    def flat(at):
        index = 0
        for a in axes:
            index = index * SIZES[a] + at[a] % SIZES[a]
        return index

    pairs = []
    for spot in itertools.product(*[range(SIZES[a]) for a in axes]):
        at = dict(zip(axes, spot))
        pairs.append((flat(at), flat({**at, **where(at)})))
    return lax.ppermute(value, axes, pairs)


def forward(at):
    return 1 if at["c"] == 0 else -1


TOKENS = ("x", "zl", "zh", "y")


def spread_over_x(grad):
    return move(grad, TOKENS, lambda at: {"x": at["x"] + at["zh"] + at["y"]})


def transpose_owner(grad):
    return move(
        grad,
        TOKENS,
        lambda at: {"zl": at["zl"] + at["y"], "zh": at["x"] - at["zh"] - at["y"], "y": at["zl"]},
    )


def positions():
    return jnp.stack([lax.axis_index(axis) for axis in ("c", "zh", "y")]).astype(jnp.int32)


def dot(a, b, dims):
    return lax.dot_general(a, b, (dims, ((), ())), preferred_element_type=jnp.float32)


def weight_kernel(at_ref, codes_ref, scales_ref, out_ref):
    half, c = out_ref.shape[-1], at_ref[0]
    cols = []
    for b in range(codes_ref.shape[1] // QBLOCK):
        scale = scales_ref[:, b : b + 1].astype(jnp.float32)
        cols.append((codes_ref[:, b * QBLOCK : (b + 1) * QBLOCK].astype(jnp.float32) * scale).astype(out_ref.dtype))
    weight = jnp.concatenate(cols, axis=1)
    out_ref[c] = weight[:, :half]
    out_ref[1 - c] = weight[:, half:]


SMEM = pl.BlockSpec(memory_space=pltpu.SMEM)
VMEM = pl.BlockSpec(memory_space=pltpu.VMEM)
LIMIT = pltpu.CompilerParams(vmem_limit_bytes=16 * MiB)


def weight_halves(at, codes, scales):
    f, width = codes.shape
    return pl.pallas_call(
        weight_kernel,
        out_shape=jax.ShapeDtypeStruct((2, f, width // 2), jnp.bfloat16),
        in_specs=[SMEM, VMEM, VMEM],
        out_specs=VMEM,
        compiler_params=LIMIT,
    )(at, codes, scales)


def hidden_grad_kernel(at_ref, own_ref, other_ref, weight_ref, out_ref):
    for g in range(own_ref.shape[0]):
        q = (g + 4 - at_ref[2]) % 4
        for x in range(weight_ref.shape[0]):
            total = dot(own_ref[g], weight_ref[x, 0], ((1,), (1,)))
            total += dot(other_ref[g], weight_ref[x, 1], ((1,), (1,)))
            out_ref[q, x] = total.astype(out_ref.dtype)


def hidden_grad_parts(at, own, other, weight):
    n, t, half = own.shape
    nx, _, f, _ = weight.shape
    return pl.pallas_call(
        hidden_grad_kernel,
        out_shape=jax.ShapeDtypeStruct((n, nx, t, f), jnp.bfloat16),
        in_specs=[SMEM] + [VMEM] * 3,
        out_specs=VMEM,
        compiler_params=LIMIT,
        cost_estimate=pl.CostEstimate(
            flops=4 * nx * n * t * f * half, bytes_accessed=4 * n * t * half, transcendentals=0
        ),
    )(at, own, other, weight)


def sum_y_kernel(got_ref, out_ref):
    for x in range(got_ref.shape[1]):
        parts = [got_ref[k, x].astype(jnp.float32) for k in range(4)]
        out_ref[x] = ((parts[0] + parts[1]) + (parts[2] + parts[3])).astype(out_ref.dtype)


def sum_y(got):
    return pl.pallas_call(
        sum_y_kernel,
        out_shape=jax.ShapeDtypeStruct(got.shape[1:], got.dtype),
        in_specs=[VMEM],
        out_specs=VMEM,
        compiler_params=LIMIT,
    )(got)


def by_distance_kernel(at_ref, got_ref, keep_ref, ahead_ref, back_ref, pass_ref):
    c, zh, y = at_ref[0], at_ref[1], at_ref[2]
    for dz, ref in ((0, keep_ref), (1 + 2 * c, ahead_ref), (3 - 2 * c, back_ref), (2, pass_ref)):
        ref[...] = got_ref[(2 * zh + dz + y) % 4]


def by_distance(at, got):
    block = jax.ShapeDtypeStruct(got.shape[1:], got.dtype)
    return pl.pallas_call(
        by_distance_kernel,
        out_shape=(block,) * 4,
        in_specs=[SMEM, VMEM],
        out_specs=(VMEM,) * 4,
        compiler_params=LIMIT,
    )(at, got)


def add_kernel(*refs):
    total = refs[0][...].astype(jnp.float32)
    for ref in refs[1:-1]:
        total += ref[...].astype(jnp.float32)
    refs[-1][...] = total.astype(refs[-1].dtype)


def add(*terms):
    return pl.pallas_call(
        add_kernel,
        out_shape=jax.ShapeDtypeStruct(terms[0].shape, terms[0].dtype),
        in_specs=[VMEM] * len(terms),
        out_specs=VMEM,
        compiler_params=LIMIT,
    )(*terms)


def weight_grad_kernel(at_ref, *refs):
    near, far, (own_ref, other_ref, out_ref) = refs[:4], refs[4:8], refs[8:]
    g, c, zh, y = pl.program_id(0), at_ref[0], at_ref[1], at_ref[2]
    q = (g + 4 - y) % 4

    @pl.when(g == 0)
    def _():
        out_ref[...] = jnp.zeros_like(out_ref)

    dy = (q + 4 - y) % 4
    side = jnp.where(dy == 0, 0, jnp.where(dy == 2, 3, jnp.where(dy == 1, 2 - c, 1 + c)))
    for x in range(own_ref.shape[0]):
        dz = (x + 12 - 2 * zh - q) % 4
        place = jnp.where(dz == 0, 0, jnp.where(dz == 2, 3, jnp.where(dz == 1, 2 - c, 1 + c)))
        hidden = [jnp.where(place < 2, near[i][place % 2], far[i][place % 2]) for i in range(4)]
        low, high = jnp.where(side == 0, hidden[0], hidden[1]), jnp.where(side == 2, hidden[2], hidden[3])
        hidden = jnp.where(side < 2, low, high)
        own, other = own_ref[x], other_ref[x]
        low = jnp.where(c == 0, own, other)
        high = jnp.where(c == 0, other, own)
        part = dot(hidden, jnp.concatenate([low, high], axis=1), ((0,), (0,)))
        for b in range(part.shape[1] // QBLOCK):
            cols = slice(b * QBLOCK, (b + 1) * QBLOCK)
            value = part[:, cols]
            s = (jnp.max(jnp.abs(value), axis=1, keepdims=True) + 1e-6).astype(jnp.bfloat16).astype(jnp.float32)
            codes = (value * (1.0 / s)).astype(jnp.bfloat16)
            out_ref[:, cols] += codes.astype(jnp.float32) * s


def weight_grad_sum(at, near, far, own, other):
    nx, n, t, half = own.shape
    f = near[0].shape[-1]
    return pl.pallas_call(
        weight_grad_kernel,
        out_shape=jax.ShapeDtypeStruct((f, 2 * half), jnp.float32),
        grid_spec=pltpu.PrefetchScalarGridSpec(
            num_scalar_prefetch=1,
            grid=(n,),
            in_specs=[pl.BlockSpec((2, t, f), lambda g, at: (0, 0, 0))] * 8
            + [pl.BlockSpec((nx, None, t, half), lambda g, at: (0, g, 0, 0))] * 2,
            out_specs=pl.BlockSpec((f, 2 * half), lambda g, at: (0, 0)),
        ),
        compiler_params=LIMIT,
        cost_estimate=pl.CostEstimate(
            flops=4 * nx * n * t * f * half, bytes_accessed=4 * nx * n * t * half, transcendentals=0
        ),
    )(at, *near, *far, own, other)


def after(value, *others):
    return lax.optimization_barrier((value, *others))[0]


def local(hidden, grad_out, weight_codes, weight_scales):
    at = positions()
    swap = lambda v: move(v, ("c",), lambda at: {"c": 1 - at["c"]})
    along = lambda v, axis, sign: move(
        v, ("c", axis) if axis != "x" else ("x", "c"), lambda at: {axis: at[axis] + sign * forward(at)}
    )
    exchange = lambda v, axis: lax.all_to_all(v, axis, split_axis=0, concat_axis=0, tiled=True)

    halves = weight_halves(at, weight_codes, weight_scales)
    weight = lax.all_gather(halves, "x", axis=0)
    hidden_back = along(hidden, "zh", 1)
    grad = transpose_owner(after(spread_over_x(grad_out), halves))
    grad = after(grad, hidden_back)
    mine = exchange(jnp.broadcast_to(grad[None], (SIZES["zl"],) + grad.shape), "zl")
    pair = jnp.stack(lax.optimization_barrier((hidden, hidden_back, grad))[:2])
    near_back, near_ahead = along(pair, "y", 1), along(pair, "y", -1)
    near = [pair, near_back, near_ahead, along(pair, "y", 2)]
    mine, weight, *near = lax.optimization_barrier((mine, weight, *near))
    mine_other = swap(mine)

    parts = hidden_grad_parts(at, mine, mine_other, weight)
    hidden_ahead = along(after(hidden, parts), "zh", -1)
    hidden_far = along(after(hidden_back, parts), "zh", 1)
    far = jnp.stack([hidden_ahead, hidden_far])
    got, far = lax.optimization_barrier((exchange(parts, "y"), far))
    far = [far, along(far, "y", 1), along(far, "y", -1), along(far, "y", 2)]
    keep, ahead, back, passing = by_distance(at, exchange(sum_y(got), "x"))
    from_ahead = along(back, "zh", -1)
    passing, *far = lax.optimization_barrier((along(passing, "zh", 1), *far))
    from_back = along(add(ahead, passing), "zh", 1)
    pieces = lax.all_gather(mine, "x", axis=0)
    weight_grad = weight_grad_sum(at, near, far, pieces, swap(after(pieces, passing)))
    from_ahead, weight_grad = lax.optimization_barrier((from_ahead, weight_grad))
    return add(keep, from_back, from_ahead), weight_grad


def solution(mesh):
    parts = Mesh(mesh.devices.reshape(tuple(SIZES.values())), tuple(SIZES))
    return jax.shard_map(
        local,
        mesh=parts,
        in_specs=(P(INNER, OUTER), P(INNER, OUTER), P(OUTER, INNER), P(OUTER, INNER)),
        out_specs=(P(INNER, OUTER), P(OUTER, INNER)),
        check_vma=False,
    )
```

```python
import itertools

import jax
import jax.numpy as jnp
from jax import lax
from jax.experimental import pallas as pl
from jax.experimental.pallas import tpu as pltpu
from jax.sharding import Mesh, PartitionSpec as P

QBLOCK = 256
SIZES = {"x": 4, "zl": 4, "c": 2, "zh": 4, "y": 4}
OUTER, INNER = ("x", "zl", "c"), ("zh", "y")
MiB = 1024 * 1024


def move(value, axes, where):
    def flat(at):
        index = 0
        for a in axes:
            index = index * SIZES[a] + at[a] % SIZES[a]
        return index

    pairs = []
    for spot in itertools.product(*[range(SIZES[a]) for a in axes]):
        at = dict(zip(axes, spot))
        pairs.append((flat(at), flat({**at, **where(at)})))
    return lax.ppermute(value, axes, pairs)


def forward(at):
    return 1 if at["c"] == 0 else -1


TOKENS = ("x", "zl", "zh", "y")


def spread_over_x(grad):
    return move(grad, TOKENS, lambda at: {"x": at["x"] + at["zh"] + at["y"]})


def transpose_owner(grad):
    return move(
        grad,
        TOKENS,
        lambda at: {"zl": at["zl"] + at["y"], "zh": at["x"] - at["zh"] - at["y"], "y": at["zl"]},
    )


def positions():
    return jnp.stack([lax.axis_index(axis) for axis in ("c", "zh", "y")]).astype(jnp.int32)


def dot(a, b, dims):
    return lax.dot_general(a, b, (dims, ((), ())), preferred_element_type=jnp.float32)


def weight_kernel(at_ref, codes_ref, scales_ref, out_ref):
    half, c = out_ref.shape[-1], at_ref[0]
    cols = []
    for b in range(codes_ref.shape[1] // QBLOCK):
        scale = scales_ref[:, b : b + 1].astype(jnp.float32)
        cols.append((codes_ref[:, b * QBLOCK : (b + 1) * QBLOCK].astype(jnp.float32) * scale).astype(out_ref.dtype))
    weight = jnp.concatenate(cols, axis=1)
    out_ref[c] = weight[:, :half]
    out_ref[1 - c] = weight[:, half:]


SMEM = pl.BlockSpec(memory_space=pltpu.SMEM)
VMEM = pl.BlockSpec(memory_space=pltpu.VMEM)
LIMIT = pltpu.CompilerParams(vmem_limit_bytes=16 * MiB)


def weight_halves(at, codes, scales):
    f, width = codes.shape
    return pl.pallas_call(
        weight_kernel,
        out_shape=jax.ShapeDtypeStruct((2, f, width // 2), jnp.bfloat16),
        in_specs=[SMEM, VMEM, VMEM],
        out_specs=VMEM,
        compiler_params=LIMIT,
    )(at, codes, scales)


def hidden_grad_kernel(at_ref, own_ref, other_ref, weight_ref, out_ref):
    for g in range(own_ref.shape[0]):
        q = (g + 4 - at_ref[2]) % 4
        for x in range(weight_ref.shape[0]):
            total = dot(own_ref[g], weight_ref[x, 0], ((1,), (1,)))
            total += dot(other_ref[g], weight_ref[x, 1], ((1,), (1,)))
            out_ref[q, x] = total.astype(out_ref.dtype)


def hidden_grad_parts(at, own, other, weight):
    n, t, half = own.shape
    nx, _, f, _ = weight.shape
    return pl.pallas_call(
        hidden_grad_kernel,
        out_shape=jax.ShapeDtypeStruct((n, nx, t, f), jnp.bfloat16),
        in_specs=[SMEM] + [VMEM] * 3,
        out_specs=VMEM,
        compiler_params=LIMIT,
        cost_estimate=pl.CostEstimate(
            flops=4 * nx * n * t * f * half, bytes_accessed=4 * n * t * half, transcendentals=0
        ),
    )(at, own, other, weight)


def sum_y_kernel(got_ref, out_ref):
    for x in range(got_ref.shape[1]):
        parts = [got_ref[k, x].astype(jnp.float32) for k in range(4)]
        out_ref[x] = ((parts[0] + parts[1]) + (parts[2] + parts[3])).astype(out_ref.dtype)


def sum_y(got):
    return pl.pallas_call(
        sum_y_kernel,
        out_shape=jax.ShapeDtypeStruct(got.shape[1:], got.dtype),
        in_specs=[VMEM],
        out_specs=VMEM,
        compiler_params=LIMIT,
    )(got)


def by_distance_kernel(at_ref, got_ref, keep_ref, ahead_ref, back_ref, pass_ref):
    c, zh, y = at_ref[0], at_ref[1], at_ref[2]
    for dz, ref in ((0, keep_ref), (1 + 2 * c, ahead_ref), (3 - 2 * c, back_ref), (2, pass_ref)):
        ref[...] = got_ref[(2 * zh + dz + y) % 4]


def by_distance(at, got):
    block = jax.ShapeDtypeStruct(got.shape[1:], got.dtype)
    return pl.pallas_call(
        by_distance_kernel,
        out_shape=(block,) * 4,
        in_specs=[SMEM, VMEM],
        out_specs=(VMEM,) * 4,
        compiler_params=LIMIT,
    )(at, got)


def add_kernel(*refs):
    total = refs[0][...].astype(jnp.float32)
    for ref in refs[1:-1]:
        total += ref[...].astype(jnp.float32)
    refs[-1][...] = total.astype(refs[-1].dtype)


def add(*terms):
    return pl.pallas_call(
        add_kernel,
        out_shape=jax.ShapeDtypeStruct(terms[0].shape, terms[0].dtype),
        in_specs=[VMEM] * len(terms),
        out_specs=VMEM,
        compiler_params=LIMIT,
    )(*terms)


def weight_grad_kernel(at_ref, *refs):
    near, far, (own_ref, other_ref, out_ref) = refs[:4], refs[4:8], refs[8:]
    g, c, zh, y = pl.program_id(0), at_ref[0], at_ref[1], at_ref[2]
    q = (g + 4 - y) % 4

    @pl.when(g == 0)
    def _():
        out_ref[...] = jnp.zeros_like(out_ref)

    dy = (q + 4 - y) % 4
    side = jnp.where(dy == 0, 0, jnp.where(dy == 2, 3, jnp.where(dy == 1, 2 - c, 1 + c)))
    for x in range(own_ref.shape[0]):
        dz = (x + 12 - 2 * zh - q) % 4
        place = jnp.where(dz == 0, 0, jnp.where(dz == 2, 3, jnp.where(dz == 1, 2 - c, 1 + c)))
        hidden = [jnp.where(place < 2, near[i][place % 2], far[i][place % 2]) for i in range(4)]
        low, high = jnp.where(side == 0, hidden[0], hidden[1]), jnp.where(side == 2, hidden[2], hidden[3])
        hidden = jnp.where(side < 2, low, high)
        own, other = own_ref[x], other_ref[x]
        low = jnp.where(c == 0, own, other)
        high = jnp.where(c == 0, other, own)
        part = dot(hidden, jnp.concatenate([low, high], axis=1), ((0,), (0,)))
        for b in range(part.shape[1] // QBLOCK):
            cols = slice(b * QBLOCK, (b + 1) * QBLOCK)
            value = part[:, cols]
            s = (jnp.max(jnp.abs(value), axis=1, keepdims=True) + 1e-6).astype(jnp.bfloat16).astype(jnp.float32)
            codes = (value * (1.0 / s)).astype(jnp.bfloat16)
            out_ref[:, cols] += codes.astype(jnp.float32) * s


def weight_grad_sum(at, near, far, own, other):
    nx, n, t, half = own.shape
    f = near[0].shape[-1]
    return pl.pallas_call(
        weight_grad_kernel,
        out_shape=jax.ShapeDtypeStruct((f, 2 * half), jnp.float32),
        grid_spec=pltpu.PrefetchScalarGridSpec(
            num_scalar_prefetch=1,
            grid=(n,),
            in_specs=[pl.BlockSpec((2, t, f), lambda g, at: (0, 0, 0))] * 8
            + [pl.BlockSpec((nx, None, t, half), lambda g, at: (0, g, 0, 0))] * 2,
            out_specs=pl.BlockSpec((f, 2 * half), lambda g, at: (0, 0)),
        ),
        compiler_params=LIMIT,
        cost_estimate=pl.CostEstimate(
            flops=4 * nx * n * t * f * half, bytes_accessed=4 * nx * n * t * half, transcendentals=0
        ),
    )(at, *near, *far, own, other)


def after(value, *others):
    return lax.optimization_barrier((value, *others))[0]


def local(hidden, grad_out, weight_codes, weight_scales):
    at = positions()
    swap = lambda v: move(v, ("c",), lambda at: {"c": 1 - at["c"]})
    along = lambda v, axis, sign: move(
        v, ("c", axis) if axis != "x" else ("x", "c"), lambda at: {axis: at[axis] + sign * forward(at)}
    )
    exchange = lambda v, axis: lax.all_to_all(v, axis, split_axis=0, concat_axis=0, tiled=True)

    halves = weight_halves(at, weight_codes, weight_scales)
    weight = lax.all_gather(halves, "x", axis=0)
    hidden_back = along(hidden, "zh", 1)
    grad = transpose_owner(after(spread_over_x(grad_out), halves))
    grad = after(grad, hidden_back)
    mine = exchange(jnp.broadcast_to(grad[None], (SIZES["zl"],) + grad.shape), "zl")
    pair = jnp.stack(lax.optimization_barrier((hidden, hidden_back, grad))[:2])
    near_back, near_ahead = along(pair, "y", 1), along(pair, "y", -1)
    near = [pair, near_back, near_ahead, along(pair, "y", 2)]
    mine, weight, *near = lax.optimization_barrier((mine, weight, *near))
    mine_other = swap(mine)

    parts = hidden_grad_parts(at, mine, mine_other, weight)
    hidden_ahead = along(after(hidden, parts), "zh", -1)
    hidden_far = along(after(hidden_back, parts), "zh", 1)
    far = jnp.stack([hidden_ahead, hidden_far])
    got, far = lax.optimization_barrier((exchange(parts, "y"), far))
    far = [far, along(far, "y", 1), along(far, "y", -1), along(far, "y", 2)]
    keep, ahead, back, passing = by_distance(at, exchange(sum_y(got), "x"))
    from_ahead = along(back, "zh", -1)
    passing, *far = lax.optimization_barrier((along(passing, "zh", 1), *far))
    from_back = along(add(ahead, passing), "zh", 1)
    pieces = lax.all_gather(mine, "x", axis=0)
    weight_grad = weight_grad_sum(at, near, far, pieces, swap(after(pieces, got)))
    from_ahead, weight_grad = lax.optimization_barrier((from_ahead, weight_grad))
    return add(keep, from_back, from_ahead), weight_grad


def solution(mesh):
    parts = Mesh(mesh.devices.reshape(tuple(SIZES.values())), tuple(SIZES))
    return jax.shard_map(
        local,
        mesh=parts,
        in_specs=(P(INNER, OUTER), P(INNER, OUTER), P(OUTER, INNER), P(OUTER, INNER)),
        out_specs=(P(INNER, OUTER), P(OUTER, INNER)),
        check_vma=False,
    )
```
